512 devices in a mesh: kv: 64 (over x, z), head: 8 (over y, core).
Axes of the slice: x: 4, y: 4, z: 16, core: 2. Of those that a mesh axis runs over, the one named last changes fastest.
Arguments:
- query_nope: bfloat16 [2, 8, 128, 128], P(None, None, 'head'), may hold values from -6 to 6
- query_rope: bfloat16 [2, 8, 128, 64], P(None, None, 'head'), may hold values from -56 to 56
- new_latent: bfloat16 [2, 8, 512], P(None, None, 'head'), may hold values from -6 to 6
- new_rope: bfloat16 [2, 8, 64], P(None, None, 'head'), may hold values from -9 to 9
- cache_latent: bfloat16 [8, 16384, 512], P(None, 'kv'), may hold values from -6 to 6
- cache_rope: bfloat16 [8, 64, 16384], P(None, None, 'kv'), may hold values from -5 to 5
- lengths: int32 [8], replicated, may hold values from 2048 to 16382
- uk_weight: bfloat16 [128, 128, 512], P('head', None, 'kv'), may hold values from -0.5 to 0.5
- uv_weight: bfloat16 [128, 512, 128], P('head'), may hold values from -0.25 to 0.25
Outputs:
- attended: bfloat16 [2, 1024, 128], P(None, ('head', 'kv'))
The draws below stay inside these ranges and needn't reach their ends.
All inputs are finite; a program needn't handle non-finite values.
Results may differ from the reference program's by a relative error of at most 0.0072.
Values may be sent and summed in bfloat16 or wider, within the bound.
No kernel may reach another device: no remote copies, remote signals or barrier semaphores. Data moves between devices by JAX's collectives and lax.ppermute only.
A program may use at most 64 MiB of HBM per device.

```python
import math
import jax
import jax.numpy as jnp
from jax import lax

HEADS = 128
NOPE = 128
ROPE = 64
LAT = 512
VD = 128
REQS = 8
STEPS = 2
CTX = 16384


def shared_rope(key):
    common = 1.3 * jnp.clip(jax.random.normal(jax.random.fold_in(key, 101), (REQS, ROPE), jnp.float32), -5.0, 5.0)
    return common


def draw_query_rope(key, part):
    common = shared_rope(key)
    key = jax.random.fold_in(key, 3)
    noise = jnp.clip(jax.random.normal(key, (STEPS, REQS, HEADS, ROPE), jnp.float32), -5.0, 5.0)
    values = common[None, :, None, :] + noise
    return values.astype(jnp.bfloat16)


def draw_new_rope(key, part):
    common = shared_rope(key)
    key = jax.random.fold_in(key, 4)
    noise = jnp.clip(jax.random.normal(key, (STEPS, REQS, ROPE), jnp.float32), -5.0, 5.0)
    values = common[None, :, :] + 0.5 * noise
    return values.astype(jnp.bfloat16)


def draw_cache_rope(key, part):
    key = jax.random.fold_in(key, 5)
    values = jnp.clip(jax.random.normal(key, (REQS, ROPE, CTX), jnp.float32), -5.0, 5.0)
    return values.astype(jnp.bfloat16)


def draw_lengths(key, part):
    key = jax.random.fold_in(key, 6)
    drawn = jax.random.randint(key, (REQS,), CTX // 8, CTX - 1)
    longest = jax.random.randint(jax.random.fold_in(key, 1), (), 0, REQS)
    return jnp.where(jnp.arange(REQS, dtype=jnp.int32) == longest, CTX - 2, drawn).astype(jnp.int32)


def block_scale(key, extent, shards, least, largest):
    level, own = 1.0, jax.random.fold_in(key, 6)
    for dim, shards_of in shards:
        steps = jnp.exp(jax.random.uniform(jax.random.fold_in(own, dim), (shards_of,), jnp.float32, least / len(shards), largest / len(shards)))
        level = level * jnp.repeat(steps, extent[dim] // shards_of).reshape([-1 if axis == dim else 1 for axis in range(len(extent))])
    return level


def centred(rng, shape, spread, bound, cuts=(), kind=jnp.bfloat16):
    values = jax.random.normal(rng, shape, jnp.float32) * spread
    if len(cuts) > 0:
        values = block_scale(rng, shape, cuts, -0.22, 0.18) * values
    return jnp.clip(values, min=-bound, max=bound).astype(kind)


def setup_inputs(seed: int = 0) -> dict:
    streams_of = jax.random.split(jax.random.key(seed), 10)
    query_nope = centred(streams_of[0], (STEPS, REQS, HEADS, NOPE), 1.0, 6.0, ((2, 8),))
    query_rope = draw_query_rope(jax.random.fold_in(streams_of[9], 71), 0)
    new_latent = centred(streams_of[2], (STEPS, REQS, LAT), 1.0, 6.0, ((2, 8),))
    new_rope = draw_new_rope(jax.random.fold_in(streams_of[9], 71), 0)
    cache_latent = centred(streams_of[4], (REQS, CTX, LAT), 1.0, 6.0, ((1, 64),))
    cache_rope = draw_cache_rope(jax.random.fold_in(streams_of[9], 71), 0)
    lengths = draw_lengths(jax.random.fold_in(streams_of[9], 71), 0)
    uk_weight = centred(streams_of[7], (HEADS, NOPE, LAT), NOPE ** -0.5, 0.5, ((0, 8), (2, 64)))
    uv_weight = centred(streams_of[8], (HEADS, LAT, VD), LAT ** -0.5, 0.25, ((0, 8),))
    return dict(query_nope=query_nope, query_rope=query_rope, new_latent=new_latent, new_rope=new_rope, cache_latent=cache_latent, cache_rope=cache_rope, lengths=lengths, uk_weight=uk_weight, uv_weight=uv_weight)


mscale = (0.1 * math.log(40.0) + 1.0) ** 2

def rounded(tensor):
    return lax.optimization_barrier(tensor.astype(jnp.bfloat16)).astype(jnp.float32)

def reference(query_nope, query_rope, new_latent, new_rope, cache_latent, cache_rope, lengths, uk_weight, uv_weight):
    single = jnp.float32
    softmax_scale = mscale / math.sqrt(NOPE + ROPE)
    query_latent = rounded(jnp.einsum('sbhn,hnl->sbhl', query_nope.astype(single), uk_weight.astype(single)))
    raw_keys = new_latent.astype(single)
    key_latent = rounded(raw_keys * lax.rsqrt(lax.optimization_barrier(jnp.mean(raw_keys * raw_keys, axis=-1, keepdims=True)) + 1e-06))
    key_rope = new_rope.astype(single)
    latent_rows = cache_latent.astype(single)
    rope_rows = cache_rope.astype(single)
    value_weight = uv_weight.astype(single)
    live_mask = jnp.arange(CTX, dtype=jnp.int32)[None, :] < lengths[:, None]
    results = []
    for step_id in range(STEPS):
        queries = query_latent[step_id]
        rotary = query_rope[step_id].astype(single)
        cached = (jnp.einsum('bhl,bjl->bhj', queries, latent_rows) + jnp.einsum('bhr,brj->bhj', rotary, rope_rows)) * softmax_scale
        cached = jnp.where(live_mask[:, None, :], cached, -1e+30)
        fresh_latent = key_latent[:step_id + 1]
        fresh_scores = (jnp.einsum('bhl,tbl->bht', queries, fresh_latent) + jnp.einsum('bhr,tbr->bht', rotary, key_rope[:step_id + 1])) * softmax_scale
        highest = jnp.maximum(lax.optimization_barrier(jnp.max(cached, axis=-1)), lax.optimization_barrier(jnp.max(fresh_scores, axis=-1)))
        weights = rounded(jnp.where(live_mask[:, None, :], jnp.exp(cached - highest[..., None]), 0.0))
        fresh_weights = rounded(jnp.exp(fresh_scores - highest[..., None]))
        totals = lax.optimization_barrier(jnp.sum(weights, axis=-1)) + lax.optimization_barrier(jnp.sum(fresh_weights, axis=-1))
        mixture = jnp.einsum('bhj,bjl->bhl', weights, latent_rows) + jnp.einsum('bht,tbl->bhl', fresh_weights, fresh_latent)
        projected = jnp.einsum('bhl,hlv->hbv', mixture, value_weight, precision=lax.Precision.HIGHEST)
        projected = projected / jnp.transpose(totals)[..., None]
        results.append(projected.reshape(HEADS * REQS, VD).astype(jnp.bfloat16))
    return jnp.stack(results)
```

```python
import math

import jax
import jax.numpy as jnp
from jax import lax
from jax.experimental import pallas as pl
from jax.experimental.pallas import tpu as pltpu
from jax.sharding import PartitionSpec as P

mscale = (0.1 * math.log(40.0) + 1.0) ** 2
f32 = jnp.float32
bf16 = jnp.bfloat16
MASKED = -1e30
LOWEST = -1e29
VM = pl.BlockSpec(memory_space=pltpu.VMEM)
SM = pl.BlockSpec(memory_space=pltpu.SMEM)
MIB = 1 << 20


def queries_kernel(q_ref, uk_ref, out_ref):
    steps, requests, heads, _ = q_ref.shape
    cols = uk_ref.shape[1]
    rows = jnp.concatenate([q_ref[s, b] for b in range(requests) for s in range(steps)], axis=0)
    weights = uk_ref[...].reshape(heads * cols, uk_ref.shape[2])
    every = lax.dot_general(
        weights, rows, (((1,), (1,)), ((), ())), preferred_element_type=f32
    ).reshape(heads, cols, rows.shape[0])
    head_of = lax.broadcasted_iota(jnp.int32, every.shape[1:], 1) % heads
    own = every[0]
    for h in range(1, heads):
        own = jnp.where(head_of == h, every[h], own)
    out_ref[...] = jnp.broadcast_to(own.astype(bf16)[None], out_ref.shape)


def rotary_kernel(scale, rel_ref, qr_ref, rope_ref, lat_new_ref, rope_new_ref, lat_ref, bias_ref, keys_ref, sem):
    requests, positions, _ = lat_ref.shape
    steps = qr_ref.shape[0]
    heads = qr_ref.shape[2]
    copy = pltpu.make_async_copy(lat_ref, keys_ref, sem)
    copy.start()
    raw = lat_new_ref[...].astype(f32)
    mean = jnp.mean(raw * raw, axis=-1, keepdims=True)
    fresh = (raw * lax.rsqrt(mean + 1e-06)).astype(bf16).astype(f32)
    turned = jnp.transpose(rope_new_ref[...].astype(f32))
    place = lax.broadcasted_iota(jnp.int32, (rope_ref.shape[1], positions), 1)
    lane = lax.broadcasted_iota(jnp.int32, (steps * heads, positions), 1)
    step_of = lax.broadcasted_iota(jnp.int32, (steps * heads, positions), 0) // heads
    for b in range(requests):
        rel = rel_ref[b]
        ropes = rope_ref[b].astype(f32)
        for t in range(steps):
            n = t * requests + b
            ropes = jnp.where(place == rel + t, turned[:, n : n + 1], ropes)
        rotary = jnp.concatenate([qr_ref[s, b] for s in range(steps)], axis=0)
        score = jnp.dot(rotary, ropes.astype(bf16), preferred_element_type=f32)
        width = steps * heads
        bias_ref[b * width : (b + 1) * width, :] = jnp.where(
            lane <= rel + step_of, score * scale, MASKED
        )
    copy.wait()
    window = 16
    row = lax.broadcasted_iota(jnp.int32, (window, lat_ref.shape[2]), 0)
    for b in range(requests):
        for t in range(steps):
            at = rel_ref[b] + t
            n = t * requests + b

            @pl.when((at >= 0) & (at < positions))
            def _():
                first = pl.multiple_of((at // window) * window, window)
                old = keys_ref[b, pl.ds(first, window), :].astype(f32)
                new = jnp.where(row == at - first, fresh[n : n + 1, :], old)
                keys_ref[b, pl.ds(first, window), :] = new.astype(bf16)


def attend_kernel(scale, q_ref, keys_ref, bias_ref, uv_ref, out_ref, mix_ref, stat_ref):
    requests, positions, _ = keys_ref.shape
    heads = uv_ref.shape[0]
    items = bias_ref.shape[0]
    width = items // requests
    tile = 128
    per_tile = tile // width
    mine = lax.broadcasted_iota(jnp.int32, (positions, tile), 1) // width
    rows_of = lax.broadcasted_iota(jnp.int32, (tile, tile), 1)
    for g in range(items // tile):
        q = q_ref[:, g * tile : (g + 1) * tile]
        scores = None
        for i in range(per_tile):
            part = jnp.dot(keys_ref[g * per_tile + i], q, preferred_element_type=f32)
            scores = part if scores is None else jnp.where(mine == i, part, scores)
        turned = jnp.transpose(scores) * scale + bias_ref[g * tile : (g + 1) * tile, :]
        highest = jnp.maximum(jnp.max(turned, axis=1, keepdims=True), LOWEST)
        weights = jnp.exp(turned - highest).astype(bf16)
        totals = jnp.maximum(jnp.sum(weights.astype(f32), axis=1, keepdims=True), 1e-30)
        level = highest + jnp.log(totals)
        inverse = 1.0 / totals
        high = level.astype(bf16).astype(f32)
        rest = level - high
        middle = rest.astype(bf16).astype(f32)
        low = rest - middle
        stat_ref[g * tile : (g + 1) * tile, :] = jnp.where(
            rows_of == 0, high, jnp.where(rows_of == 1, middle, jnp.where(rows_of == 2, low, 0.0))
        )
        for i in range(per_tile):
            b = g * per_tile + i
            mix = jnp.dot(
                weights[i * width : (i + 1) * width], keys_ref[b], preferred_element_type=f32
            )
            mix = mix * inverse[i * width : (i + 1) * width]
            for c in range(mix_ref.shape[0]):
                mix_ref[c, b * width : (b + 1) * width, :] = mix[:, c * tile : (c + 1) * tile]
    each = items // heads
    upper = lax.broadcasted_iota(jnp.int32, (8, tile), 0) < 4
    for h in range(heads):
        mixed = jnp.concatenate(
            [mix_ref[c, pl.ds(h, each, stride=heads), :] for c in range(mix_ref.shape[0])], axis=1
        ).astype(bf16)
        stats = stat_ref[pl.ds(h, each, stride=heads), :]
        projected = jnp.dot(mixed, uv_ref[h], preferred_element_type=f32)
        for v in range(each // 8):
            p = projected[v * 8 : (v + 1) * 8]
            st = stats[v * 8 : (v + 1) * 8]
            first = h * (each // 4) + 2 * v
            out_ref[first] = jnp.where(upper, p, pltpu.roll(st, 4, 0)).astype(bf16)
            out_ref[first + 1] = jnp.where(upper, pltpu.roll(p, 4, 0), st).astype(bf16)


def merge_kernel(parts_ref, out_ref):
    parts = parts_ref[...].astype(f32)
    levels = jnp.sum(parts, axis=2, keepdims=True)
    factor = jnp.exp(levels - jnp.max(levels, axis=0, keepdims=True))
    values = pltpu.roll(parts, 4, 1)
    merged = jnp.sum(values * factor, axis=0) / jnp.sum(factor, axis=0)
    steps, owned, _ = out_ref.shape
    for s in range(steps):
        rows = [merged[4 + i * steps + s : 5 + i * steps + s] for i in range(owned)]
        out_ref[s] = jnp.concatenate(rows, axis=0).astype(bf16)


def exchange(array):
    return lax.all_to_all(array, "kv", split_axis=0, concat_axis=0, tiled=True)


def gather_heads(block):
    count = lax.axis_size("head")
    me = lax.axis_index("head")
    held = block[None]
    bit = 1
    while bit < count:
        other = lax.ppermute(held, "head", [(i, i ^ bit) for i in range(count)])
        upper = (me & bit) != 0
        held = jnp.concatenate(
            [jnp.where(upper, other, held), jnp.where(upper, held, other)], axis=0
        )
        bit *= 2
    return held


def absorbed(query_nope, uk_weight, shards):
    steps, requests, heads, _ = query_nope.shape
    cols = uk_weight.shape[2]
    return pl.pallas_call(
        queries_kernel,
        out_shape=jax.ShapeDtypeStruct((shards, cols, steps * requests * heads), bf16),
        in_specs=[VM, VM],
        out_specs=VM,
    )(query_nope, jnp.swapaxes(uk_weight, 1, 2))


def prepare(scale, rel, query_rope, cache_rope, lat_new, rope_new, cache_latent):
    steps, requests, heads, _ = query_rope.shape
    positions = cache_latent.shape[1]
    return pl.pallas_call(
        lambda *refs: rotary_kernel(scale, *refs),
        out_shape=(
            jax.ShapeDtypeStruct((steps * requests * heads, positions), f32),
            jax.ShapeDtypeStruct(cache_latent.shape, bf16),
        ),
        in_specs=[SM, VM, VM, VM, VM, pl.BlockSpec(memory_space=pl.ANY)],
        out_specs=(VM, VM),
        scratch_shapes=[pltpu.SemaphoreType.DMA],
        compiler_params=pltpu.CompilerParams(vmem_limit_bytes=16 * MIB),
    )(rel, query_rope, cache_rope, lat_new, rope_new, cache_latent)


def attend(scale, queries, keys, bias, uv_weight, shards):
    items = bias.shape[0]
    heads, lat, vd = uv_weight.shape
    return pl.pallas_call(
        lambda *refs: attend_kernel(scale, *refs),
        out_shape=jax.ShapeDtypeStruct((shards, 8, vd), bf16),
        in_specs=[VM] * 4,
        out_specs=VM,
        scratch_shapes=[pltpu.VMEM((lat // 128, items, 128), f32), pltpu.VMEM((items, 128), f32)],
        compiler_params=pltpu.CompilerParams(vmem_limit_bytes=24 * MIB),
    )(queries, keys, bias, uv_weight)


def merge(parts, steps, owned):
    return pl.pallas_call(
        merge_kernel,
        out_shape=jax.ShapeDtypeStruct((steps, owned, parts.shape[2]), bf16),
        in_specs=[VM],
        out_specs=VM,
    )(parts)


def on_device(
    query_nope,
    query_rope,
    new_latent,
    new_rope,
    cache_latent,
    cache_rope,
    lengths,
    uk_weight,
    uv_weight,
):
    shards = lax.axis_size("kv")
    steps, requests, heads, nope = query_nope.shape
    positions = cache_latent.shape[1]
    scale = mscale / math.sqrt(nope + query_rope.shape[3])
    columns = exchange(absorbed(query_nope, uk_weight, shards))
    queries = columns.reshape(-1, columns.shape[2])
    mine = jnp.concatenate([new_latent, new_rope], axis=2).reshape(steps * requests, -1)
    tokens = jnp.swapaxes(gather_heads(mine), 0, 1)
    width = new_latent.shape[2]
    lat_new = tokens[:, :, :width].reshape(steps * requests, -1)
    rope_new = tokens[:, :, width:].reshape(steps * requests, -1)
    rel = lengths - lax.axis_index("kv") * positions
    bias, keys = prepare(scale, rel, query_rope, cache_rope, lat_new, rope_new, cache_latent)
    parts = attend(scale, queries, keys, bias, uv_weight, shards)
    return merge(exchange(parts), steps, heads * requests // shards)


def solution(mesh):
    return jax.shard_map(
        on_device,
        mesh=mesh,
        in_specs=(
            P(None, None, "head", None),
            P(None, None, "head", None),
            P(None, None, "head"),
            P(None, None, "head"),
            P(None, "kv", None),
            P(None, None, "kv"),
            P(),
            P("head", None, "kv"),
            P("head", None, None),
        ),
        out_specs=P(None, ("head", "kv"), None),
        check_vma=False,
    )
```

```python
import math

import jax
import jax.numpy as jnp
from jax import lax
from jax.experimental import pallas as pl
from jax.experimental.pallas import tpu as pltpu
from jax.sharding import PartitionSpec as P

mscale = (0.1 * math.log(40.0) + 1.0) ** 2
f32 = jnp.float32
bf16 = jnp.bfloat16
MASKED = -1e30
LOWEST = -1e29
VM = pl.BlockSpec(memory_space=pltpu.VMEM)
SM = pl.BlockSpec(memory_space=pltpu.SMEM)
HBM = pl.BlockSpec(memory_space=pltpu.HBM)
RINGS = 4
ALONG, ACROSS, ALL = 10, 2, 42


def fetch(*copies):
    copies = [pltpu.make_async_copy(*copy) for copy in copies]
    for copy in copies:
        copy.start()
    for copy in copies:
        copy.wait()


def queries_kernel(q_hbm, uk_hbm, out_ref, q_ref, uk_ref, sems):
    fetch((uk_hbm, uk_ref, sems.at[0]), (q_hbm, q_ref, sems.at[1]))
    steps, requests, heads, _ = q_ref.shape
    cols = uk_ref.shape[1]
    rows = jnp.concatenate([q_ref[s, b] for b in range(requests) for s in range(steps)], axis=0)
    weights = uk_ref[...].reshape(heads * cols, uk_ref.shape[2])
    every = lax.dot_general(
        weights, rows, (((1,), (1,)), ((), ())), preferred_element_type=f32
    ).reshape(heads, cols, rows.shape[0])
    head_of = lax.broadcasted_iota(jnp.int32, every.shape[1:], 1) % heads
    own = every[0]
    for h in range(1, heads):
        own = jnp.where(head_of == h, every[h], own)
    out_ref[...] = jnp.broadcast_to(own.astype(bf16)[None], out_ref.shape)


def repeat_kernel(shift, in_ref, *refs):
    out_ref = refs[-1]
    count, cols, items = in_ref.shape
    rows = in_ref[...].reshape(count * cols, items)
    first = (count - shift) * cols
    ordered = jnp.concatenate([rows[first:], rows[:first]], axis=0)
    out_ref[...] = jnp.broadcast_to(ordered[None], out_ref.shape)


def tokens_kernel(lat_hbm, rope_hbm, _, out_ref, lat_ref, rope_ref, sems):
    fetch((lat_hbm, lat_ref, sems.at[0]), (rope_hbm, rope_ref, sems.at[1]))
    steps, requests, lat = lat_ref.shape
    rope = rope_ref.shape[2]
    rows = steps * requests

    def one_hot(shape, shift):
        return (
            lax.broadcasted_iota(jnp.int32, shape, 1) == lax.broadcasted_iota(jnp.int32, shape, 0) + shift
        ).astype(bf16)

    def joined(ref):
        return jnp.concatenate([ref[t] for t in range(steps)], axis=0)

    placed = jnp.dot(joined(lat_ref), one_hot((lat, 128), 64), preferred_element_type=f32)
    placed += jnp.dot(joined(rope_ref), one_hot((rope, 128), 8), preferred_element_type=f32)
    to = lax.broadcasted_iota(jnp.int32, (rows, rows), 0)
    source = lax.broadcasted_iota(jnp.int32, (rows, rows), 1)
    order = ((to % steps) * requests + to // steps == source).astype(bf16)
    out_ref[...] = jnp.dot(order, placed.astype(bf16), preferred_element_type=f32).astype(bf16)


def own_rows(shard, items, requests, heads, steps):
    row = lax.broadcasted_iota(jnp.int32, (8, items), 0) - 4
    item = lax.broadcasted_iota(jnp.int32, (8, items), 1)
    owned = 4 // steps
    groups = requests // owned
    request = owned * (shard % groups) + row // steps
    wanted = request * (steps * heads) + (row % steps) * heads + shard // groups
    return ((row >= 0) & (item == wanted)).astype(bf16)


def prepare_kernel(
    scale, place_ref, length_ref, qr_hbm, rope_hbm, keys_hbm, uv_hbm, _,
    bias_ref, own_ref, keys_ref, uv_own_ref, qr_ref, rope_ref, sems,
):
    steps, requests, heads, ropes = qr_ref.shape
    shard = place_ref[0]
    owner = shard // (requests // (4 // steps))
    pairs = [
        (rope_hbm, rope_ref), (qr_hbm, qr_ref), (keys_hbm, keys_ref), (uv_hbm.at[owner], uv_own_ref),
    ]
    copies = [pltpu.make_async_copy(p, q, sems.at[i]) for i, (p, q) in enumerate(pairs)]
    for copy in copies:
        copy.start()
    copies[0].wait()
    copies[1].wait()
    positions = rope_ref.shape[2]
    width = steps * heads
    lane = lax.broadcasted_iota(jnp.int32, (width, positions), 1) + shard * positions
    rows = [
        jnp.concatenate([qr_ref[s, b] for s in range(steps)], axis=0) for b in range(requests)
    ]
    for b in range(requests):
        score = jnp.dot(rows[b], rope_ref[b], preferred_element_type=f32)
        bias_ref[b * width : (b + 1) * width, :] = jnp.where(
            lane < length_ref[b], score * scale, MASKED
        )
    every = jnp.concatenate(rows, axis=0)
    own = own_rows(shard, width * requests, requests, heads, steps)
    mine = jnp.dot(own, every, preferred_element_type=f32).astype(bf16)
    groups = own_ref.shape[0]
    each = ropes // groups
    at = lax.broadcasted_iota(jnp.int32, (ropes, 128), 0)
    to = lax.broadcasted_iota(jnp.int32, (ropes, 128), 1)
    for g in range(groups):
        spread = (at == to - 8 + each * g) & (to >= 8) & (to < 8 + each)
        own_ref[g] = jnp.dot(mine, spread.astype(bf16), preferred_element_type=f32)
    for copy in copies[2:]:
        copy.wait()


def attend_kernel(
    scale, turn, shift, place_ref, q_ref, keys_ref, bias_ref, uv_hbm, token_ref,
    out_ref, own_ref, mix_ref, stat_ref, uv_ref, sem,
):
    copy = pltpu.make_async_copy(uv_hbm, uv_ref, sem)
    copy.start()
    requests, positions, _ = keys_ref.shape
    heads = uv_ref.shape[0]
    items = bias_ref.shape[0]
    width = items // requests
    tile = 128
    per_tile = tile // width
    mine = lax.broadcasted_iota(jnp.int32, (positions, tile), 1) // width
    rows_of = lax.broadcasted_iota(jnp.int32, (tile, tile), 1)
    rings = q_ref.shape[0]
    queries = jnp.concatenate([q_ref[(i - turn) % rings] for i in range(rings)], axis=0)
    for g in range(items // tile):
        q = queries[:, g * tile : (g + 1) * tile]
        scores = None
        for i in range(per_tile):
            part = jnp.dot(keys_ref[g * per_tile + i], q, preferred_element_type=f32)
            scores = part if scores is None else jnp.where(mine == i, part, scores)
        turned = jnp.transpose(scores) * scale + bias_ref[g * tile : (g + 1) * tile, :]
        highest = jnp.maximum(jnp.max(turned, axis=1, keepdims=True), LOWEST)
        weights = jnp.exp(turned - highest).astype(bf16)
        totals = jnp.maximum(jnp.sum(weights.astype(f32), axis=1, keepdims=True), 1e-30)
        level = highest + jnp.log(totals)
        inverse = 1.0 / totals
        high = level.astype(bf16).astype(f32)
        rest = level - high
        middle = rest.astype(bf16).astype(f32)
        low = rest - middle
        stat_ref[g * tile : (g + 1) * tile, :] = jnp.where(
            rows_of == 0, high, jnp.where(rows_of == 1, middle, jnp.where(rows_of == 2, low, 0.0))
        )
        for i in range(per_tile):
            b = g * per_tile + i
            mix = jnp.dot(
                weights[i * width : (i + 1) * width], keys_ref[b], preferred_element_type=f32
            )
            mix = mix * inverse[i * width : (i + 1) * width]
            for c in range(mix_ref.shape[0]):
                mix_ref[c, b * width : (b + 1) * width, :] = mix[:, c * tile : (c + 1) * tile]
    each = items // heads
    own = own_rows(place_ref[0], items, requests, heads, width // heads)
    own_ref[...] = lax.dot_general(
        own, queries, (((1,), (1,)), ((), ())), preferred_element_type=f32
    )
    token = token_ref[...].astype(f32)
    copy.wait()
    upper = lax.broadcasted_iota(jnp.int32, (8, tile), 0) < 4
    for h in range(heads):
        mixed = jnp.concatenate(
            [mix_ref[c, pl.ds(h, each, stride=heads), :] for c in range(mix_ref.shape[0])], axis=1
        ).astype(bf16)
        stats = stat_ref[pl.ds(h, each, stride=heads), :] + token
        projected = jnp.dot(mixed, uv_ref[h], preferred_element_type=f32)
        for v in range(each // 8):
            p = projected[v * 8 : (v + 1) * 8]
            st = stats[v * 8 : (v + 1) * 8]
            first = h * (each // 4) + 2 * v
            shards = out_ref.shape[0]
            out_ref[(first - shift) % shards] = jnp.where(upper, p, pltpu.roll(st, 4, 0)).astype(bf16)
            out_ref[(first + 1 - shift) % shards] = jnp.where(upper, pltpu.roll(p, 4, 0), st).astype(bf16)


def merge_kernel(scale, shift, place_ref, parts_ref, q_ref, rope_ref, uv_ref, out_ref):
    steps, owned, _ = out_ref.shape
    groups = rope_ref.shape[0]
    parts = parts_ref[...].astype(f32)
    lanes = lax.broadcasted_iota(jnp.int32, parts.shape, 2)
    levels = jnp.sum(jnp.where(lanes < 3, parts, 0.0), axis=2, keepdims=True)
    lane = lanes[0]
    row = lax.broadcasted_iota(jnp.int32, (8, 1), 0)
    blocks = [
        parts_ref[(g + groups - place_ref[1]) % groups + parts.shape[0] - shift].astype(f32)
        for g in range(groups)
    ]
    raw = jnp.concatenate(
        [
            jnp.where(lane < 64, pltpu.roll(blocks[g], 64, 1), blocks[g + 1])
            for g in range(0, groups, 2)
        ],
        axis=1,
    )
    mean = jnp.mean(raw * raw, axis=1, keepdims=True)
    key = (raw * lax.rsqrt(mean + 1e-06)).astype(bf16)
    value = jnp.dot(key, uv_ref[...], preferred_element_type=f32)
    key = key.astype(f32)
    queries = q_ref[...]

    def score(back):
        ropes = sum(pltpu.roll(blocks[g], back, 0) * rope_ref[g] for g in range(groups))
        latent = jnp.sum(pltpu.roll(key, back, 0) * queries, axis=1, keepdims=True)
        return (latent + jnp.sum(ropes, axis=1, keepdims=True)) * scale

    summit = jnp.max(levels, axis=0)
    fresh = []
    for back in range(steps):
        level = jnp.where(row % steps >= back, score(back), MASKED)
        fresh.append((level, pltpu.roll(value, back, 0)))
        summit = jnp.maximum(summit, level)
    factor = jnp.exp(levels - summit[None])
    merged = jnp.sum(pltpu.roll(parts, 4, 1) * factor, axis=0)
    totals = jnp.sum(factor, axis=0)
    for level, values in fresh:
        factor = jnp.exp(level - summit)
        merged += factor * values
        totals += factor
    merged = merged / totals
    for s in range(steps):
        rows = [merged[4 + i * steps + s : 5 + i * steps + s] for i in range(owned)]
        out_ref[s] = jnp.concatenate(rows, axis=0).astype(bf16)


def exchange(array, groups):
    return lax.all_to_all(
        array, "kv", split_axis=0, concat_axis=0, tiled=True, axis_index_groups=groups
    )


def spread_tokens(block):
    shards, groups = lax.axis_size("kv"), lax.axis_size("head")
    pairs = [
        (k * groups + (g + k) % groups, k * groups + g) for k in range(shards) for g in range(groups)
    ]
    return lax.ppermute(block, ("kv", "head"), pairs)


def near(shape, kind):
    return pltpu.VMEM(shape, kind)


def pinned(space, *arrays):
    return [pltpu.with_memory_space_constraint(array, space) for array in arrays]


def limit(mib):
    return pltpu.CompilerParams(vmem_limit_bytes=mib << 20)


def cost(flops, moved):
    return pl.CostEstimate(flops=flops, bytes_accessed=moved, transcendentals=0)


def absorbed(query_nope, uk_weight, copies):
    steps, requests, heads, _ = query_nope.shape
    uk = jnp.swapaxes(uk_weight, 1, 2)
    return pl.pallas_call(
        queries_kernel,
        out_shape=jax.ShapeDtypeStruct((copies, uk.shape[1], steps * requests * heads), bf16),
        in_specs=[HBM, HBM],
        out_specs=VM,
        scratch_shapes=[
            pltpu.VMEM(query_nope.shape, bf16),
            pltpu.VMEM(uk.shape, bf16),
            pltpu.SemaphoreType.DMA((2,)),
        ],
        compiler_params=limit(4),
    )(*pinned(pltpu.HBM, query_nope, uk))


def repeated(columns, shift, copies, *after):
    count, cols, items = columns.shape
    return pl.pallas_call(
        lambda *refs: repeat_kernel(shift, *refs),
        out_shape=jax.ShapeDtypeStruct((copies, count * cols, items), bf16),
        in_specs=[VM] + [pl.BlockSpec(memory_space=pl.ANY)] * len(after),
        out_specs=VM,
        compiler_params=limit(4),
    )(columns, *after)


def tokens(new_latent, new_rope, after):
    rows = new_latent.shape[0] * new_latent.shape[1]
    return pl.pallas_call(
        tokens_kernel,
        out_shape=jax.ShapeDtypeStruct((rows, 128), bf16),
        in_specs=[HBM, HBM, pl.BlockSpec(memory_space=pl.ANY)],
        out_specs=VM,
        scratch_shapes=[
            pltpu.VMEM(new_latent.shape, bf16),
            pltpu.VMEM(new_rope.shape, bf16),
            pltpu.SemaphoreType.DMA((2,)),
        ],
        compiler_params=limit(4),
        cost_estimate=cost(1 << 20, 1 << 16),
    )(*pinned(pltpu.HBM, new_latent, new_rope), after)


def prepare(scale, place, lengths, query_rope, cache_rope, cache_latent, uv_weight, after, groups):
    steps, requests, heads, _ = query_rope.shape
    positions = cache_rope.shape[2]
    return pl.pallas_call(
        lambda *refs: prepare_kernel(scale, *refs),
        out_shape=(
            near((steps * requests * heads, positions), f32),
            near((groups, 8, 128), f32),
            near(cache_latent.shape, bf16),
            near(uv_weight.shape[1:], bf16),
        ),
        in_specs=[SM, SM] + [HBM] * 4 + [pl.BlockSpec(memory_space=pl.ANY)],
        out_specs=(VM,) * 4,
        scratch_shapes=[
            pltpu.VMEM(query_rope.shape, bf16),
            pltpu.VMEM(cache_rope.shape, bf16),
            pltpu.SemaphoreType.DMA((4,)),
        ],
        compiler_params=limit(16),
        cost_estimate=cost(1 << 28, 1 << 22),
    )(
        place,
        lengths,
        *pinned(pltpu.HBM, query_rope, cache_rope, cache_latent, uv_weight),
        after,
    )


def attend(scale, turn, shift, place, queries, keys, bias, uv_weight, token, shards):
    items = bias.shape[0]
    heads, lat, vd = uv_weight.shape
    return pl.pallas_call(
        lambda *refs: attend_kernel(scale, turn, shift, *refs),
        out_shape=(
            jax.ShapeDtypeStruct((shards, 8, vd), bf16),
            jax.ShapeDtypeStruct((8, lat), f32),
        ),
        in_specs=[SM, VM, VM, VM, HBM, VM],
        out_specs=(VM, VM),
        scratch_shapes=[
            pltpu.VMEM((lat // 128, items, 128), f32),
            pltpu.VMEM((items, 128), f32),
            pltpu.VMEM(uv_weight.shape, bf16),
            pltpu.SemaphoreType.DMA,
        ],
        compiler_params=limit(16),
    )(place, queries, *pinned(pltpu.VMEM, keys, bias), *pinned(pltpu.HBM, uv_weight), token)


def merge(scale, shift, place, parts, queries, ropes, uv_own, steps, owned):
    return pl.pallas_call(
        lambda *refs: merge_kernel(scale, shift, *refs),
        out_shape=jax.ShapeDtypeStruct((steps, owned, parts.shape[2]), bf16),
        in_specs=[SM] + [VM] * 4,
        out_specs=VM,
        compiler_params=limit(8),
    )(place, parts, queries, ropes, uv_own)


def on_device(
    query_nope,
    query_rope,
    new_latent,
    new_rope,
    cache_latent,
    cache_rope,
    lengths,
    uk_weight,
    uv_weight,
):
    shards, groups = lax.axis_size("kv"), lax.axis_size("head")
    steps, requests, heads, nope = query_nope.shape
    owned = heads * requests // shards
    scale = mscale / math.sqrt(nope + query_rope.shape[3])
    place = jnp.stack([lax.axis_index("kv"), lax.axis_index("head")]).astype(jnp.int32)
    rings = RINGS
    size = shards // rings
    along = [[r * size + (i + ALONG) % size for i in range(size)] for r in range(rings)]
    across = [[(i + ACROSS) % rings * size + p for i in range(rings)] for p in range(size)]
    everyone = [[(i + ALL) % shards for i in range(shards)]]
    block = absorbed(query_nope, uk_weight, size)
    ring = exchange(block, along)
    token = spread_tokens(tokens(new_latent, new_rope, block))
    bias, ropes, keys, uv_own = prepare(
        scale, place, lengths, query_rope, cache_rope, cache_latent, uv_weight, block, groups
    )
    queries = exchange(repeated(ring, ALONG, rings, ropes, token), across)
    parts, own = attend(scale, ACROSS, ALL, place, queries, keys, bias, uv_weight, token, shards)
    parts = exchange(parts, everyone)
    return merge(scale, ALL, place, parts, own, ropes, uv_own, steps, owned)


def solution(mesh):
    return jax.shard_map(
        on_device,
        mesh=mesh,
        in_specs=(
            P(None, None, "head", None),
            P(None, None, "head", None),
            P(None, None, "head"),
            P(None, None, "head"),
            P(None, "kv", None),
            P(None, None, "kv"),
            P(),
            P("head", None, "kv"),
            P("head", None, None),
        ),
        out_specs=P(None, ("head", "kv"), None),
        check_vma=False,
    )
```

```python
import math

import jax
import jax.numpy as jnp
from jax import lax
from jax.experimental import pallas as pl
from jax.experimental.pallas import tpu as pltpu
from jax.sharding import PartitionSpec as P

mscale = (0.1 * math.log(40.0) + 1.0) ** 2
f32 = jnp.float32
bf16 = jnp.bfloat16
MASKED = -1e30
LOWEST = -1e29
VM = pl.BlockSpec(memory_space=pltpu.VMEM)
SM = pl.BlockSpec(memory_space=pltpu.SMEM)
HBM = pl.BlockSpec(memory_space=pltpu.HBM)
RINGS = 4
ALONG, ACROSS, ALL = 10, 2, 40


def fetch(*copies):
    copies = [pltpu.make_async_copy(*copy) for copy in copies]
    for copy in copies:
        copy.start()
    for copy in copies:
        copy.wait()


def queries_kernel(q_hbm, uk_hbm, out_ref, q_ref, uk_ref, sems):
    fetch((uk_hbm, uk_ref, sems.at[0]), (q_hbm, q_ref, sems.at[1]))
    steps, requests, heads, _ = q_ref.shape
    cols = uk_ref.shape[1]
    rows = jnp.concatenate([q_ref[s, b] for b in range(requests) for s in range(steps)], axis=0)
    weights = uk_ref[...].reshape(heads * cols, uk_ref.shape[2])
    every = lax.dot_general(
        weights, rows, (((1,), (1,)), ((), ())), preferred_element_type=f32
    ).reshape(heads, cols, rows.shape[0])
    head_of = lax.broadcasted_iota(jnp.int32, every.shape[1:], 1) % heads
    own = every[0]
    for h in range(1, heads):
        own = jnp.where(head_of == h, every[h], own)
    out_ref[...] = jnp.broadcast_to(own.astype(bf16)[None], out_ref.shape)


def repeat_kernel(shift, in_ref, *refs):
    out_ref = refs[-1]
    count, cols, items = in_ref.shape
    rows = in_ref[...].reshape(count * cols, items)
    first = (count - shift) * cols
    ordered = jnp.concatenate([rows[first:], rows[:first]], axis=0)
    out_ref[...] = jnp.broadcast_to(ordered[None], out_ref.shape)


def put_tokens(lat_ref, rope_ref, out_ref):
    steps, requests, lat = lat_ref.shape
    rope = rope_ref.shape[2]
    rows = steps * requests

    def one_hot(shape, shift):
        return (
            lax.broadcasted_iota(jnp.int32, shape, 1) == lax.broadcasted_iota(jnp.int32, shape, 0) + shift
        ).astype(bf16)

    def joined(ref):
        return jnp.concatenate([ref[t] for t in range(steps)], axis=0)

    placed = jnp.dot(joined(lat_ref), one_hot((lat, 128), 64), preferred_element_type=f32)
    placed += jnp.dot(joined(rope_ref), one_hot((rope, 128), 8), preferred_element_type=f32)
    to = lax.broadcasted_iota(jnp.int32, (rows, rows), 0)
    source = lax.broadcasted_iota(jnp.int32, (rows, rows), 1)
    order = ((to % steps) * requests + to // steps == source).astype(bf16)
    out_ref[...] = jnp.dot(order, placed.astype(bf16), preferred_element_type=f32).astype(bf16)


def own_rows(shard, items, requests, heads, steps):
    row = lax.broadcasted_iota(jnp.int32, (8, items), 0) - 4
    item = lax.broadcasted_iota(jnp.int32, (8, items), 1)
    owned = 4 // steps
    groups = requests // owned
    request = owned * (shard % groups) + row // steps
    wanted = request * (steps * heads) + (row % steps) * heads + shard // groups
    return ((row >= 0) & (item == wanted)).astype(bf16)


def prepare_kernel(
    scale, place_ref, length_hbm, qr_hbm, rope_hbm, keys_hbm, uv_hbm, lat_new_hbm, rope_new_hbm, _,
    bias_ref, own_ref, keys_ref, uv_own_ref, token_ref,
    length_ref, qr_ref, rope_ref, lat_new_ref, rope_new_ref, sems,
):
    steps, requests, heads, ropes = qr_ref.shape
    shard = place_ref[0]
    owner = shard // (requests // (4 // steps))
    pairs = [
        (lat_new_hbm, lat_new_ref), (rope_new_hbm, rope_new_ref), (length_hbm, length_ref),
        (qr_hbm, qr_ref), (rope_hbm, rope_ref), (keys_hbm, keys_ref), (uv_hbm.at[owner], uv_own_ref),
    ]
    copies = [pltpu.make_async_copy(p, q, sems.at[i]) for i, (p, q) in enumerate(pairs)]
    for copy in copies:
        copy.start()
    for copy in copies[:5]:
        copy.wait()
    put_tokens(lat_new_ref, rope_new_ref, token_ref)
    positions = rope_ref.shape[2]
    width = steps * heads
    lane = lax.broadcasted_iota(jnp.int32, (width, positions), 1) + shard * positions
    rows = [
        jnp.concatenate([qr_ref[s, b] for s in range(steps)], axis=0) for b in range(requests)
    ]
    for b in range(requests):
        score = jnp.dot(rows[b], rope_ref[b], preferred_element_type=f32)
        bias_ref[b * width : (b + 1) * width, :] = jnp.where(
            lane < length_ref[b], score * scale, MASKED
        )
    every = jnp.concatenate(rows, axis=0)
    own = own_rows(shard, width * requests, requests, heads, steps)
    mine = jnp.dot(own, every, preferred_element_type=f32).astype(bf16)
    groups = own_ref.shape[0]
    each = ropes // groups
    at = lax.broadcasted_iota(jnp.int32, (ropes, 128), 0)
    to = lax.broadcasted_iota(jnp.int32, (ropes, 128), 1)
    for g in range(groups):
        spread = (at == to - 8 + each * g) & (to >= 8) & (to < 8 + each)
        own_ref[g] = jnp.dot(mine, spread.astype(bf16), preferred_element_type=f32)
    for copy in copies[5:]:
        copy.wait()


def attend_kernel(
    scale, turn, shift, place_ref, q_ref, keys_ref, bias_ref, uv_hbm, token_ref,
    out_ref, own_ref, mix_ref, stat_ref, uv_ref, sem,
):
    copy = pltpu.make_async_copy(uv_hbm, uv_ref, sem)
    copy.start()
    requests, positions, _ = keys_ref.shape
    heads = uv_ref.shape[0]
    items = bias_ref.shape[0]
    width = items // requests
    tile = 128
    per_tile = tile // width
    mine = lax.broadcasted_iota(jnp.int32, (positions, tile), 1) // width
    rows_of = lax.broadcasted_iota(jnp.int32, (tile, tile), 1)
    rings = q_ref.shape[0]
    queries = jnp.concatenate([q_ref[(i - turn) % rings] for i in range(rings)], axis=0)
    for g in range(items // tile):
        q = queries[:, g * tile : (g + 1) * tile]
        scores = None
        for i in range(per_tile):
            part = jnp.dot(keys_ref[g * per_tile + i], q, preferred_element_type=f32)
            scores = part if scores is None else jnp.where(mine == i, part, scores)
        turned = jnp.transpose(scores) * scale + bias_ref[g * tile : (g + 1) * tile, :]
        highest = jnp.maximum(jnp.max(turned, axis=1, keepdims=True), LOWEST)
        weights = jnp.exp(turned - highest).astype(bf16)
        totals = jnp.maximum(jnp.sum(weights.astype(f32), axis=1, keepdims=True), 1e-30)
        level = highest + jnp.log(totals)
        inverse = 1.0 / totals
        high = level.astype(bf16).astype(f32)
        rest = level - high
        middle = rest.astype(bf16).astype(f32)
        low = rest - middle
        stat_ref[g * tile : (g + 1) * tile, :] = jnp.where(
            rows_of == 0, high, jnp.where(rows_of == 1, middle, jnp.where(rows_of == 2, low, 0.0))
        )
        for i in range(per_tile):
            b = g * per_tile + i
            mix = jnp.dot(
                weights[i * width : (i + 1) * width], keys_ref[b], preferred_element_type=f32
            )
            mix = mix * inverse[i * width : (i + 1) * width]
            for c in range(mix_ref.shape[0]):
                mix_ref[c, b * width : (b + 1) * width, :] = mix[:, c * tile : (c + 1) * tile]
    each = items // heads
    own = own_rows(place_ref[0], items, requests, heads, width // heads)
    own_ref[...] = lax.dot_general(
        own, queries, (((1,), (1,)), ((), ())), preferred_element_type=f32
    )
    token = token_ref[...].astype(f32)
    copy.wait()
    upper = lax.broadcasted_iota(jnp.int32, (8, tile), 0) < 4
    for h in range(heads):
        mixed = jnp.concatenate(
            [mix_ref[c, pl.ds(h, each, stride=heads), :] for c in range(mix_ref.shape[0])], axis=1
        ).astype(bf16)
        stats = stat_ref[pl.ds(h, each, stride=heads), :] + token
        projected = jnp.dot(mixed, uv_ref[h], preferred_element_type=f32)
        for v in range(each // 8):
            p = projected[v * 8 : (v + 1) * 8]
            st = stats[v * 8 : (v + 1) * 8]
            first = h * (each // 4) + 2 * v
            shards = out_ref.shape[0]
            out_ref[(first - shift) % shards] = jnp.where(upper, p, pltpu.roll(st, 4, 0)).astype(bf16)
            out_ref[(first + 1 - shift) % shards] = jnp.where(upper, pltpu.roll(p, 4, 0), st).astype(bf16)


def merge_kernel(scale, shift, place_ref, parts_ref, q_ref, rope_ref, uv_ref, out_ref):
    steps, owned, _ = out_ref.shape
    groups = rope_ref.shape[0]
    parts = parts_ref[...].astype(f32)
    shards = parts.shape[0]
    lanes = lax.broadcasted_iota(jnp.int32, parts.shape, 2)
    levels = jnp.sum(jnp.where(lanes < 3, parts, 0.0), axis=2, keepdims=True)
    lane = lanes[0]
    row = lax.broadcasted_iota(jnp.int32, (8, 1), 0)
    blocks = [
        parts_ref[
            (holder((g + groups - place_ref[1]) % groups, shards // RINGS) + shards - shift) % shards
        ].astype(f32)
        for g in range(groups)
    ]
    raw = jnp.concatenate(
        [
            jnp.where(lane < 64, pltpu.roll(blocks[g], 64, 1), blocks[g + 1])
            for g in range(0, groups, 2)
        ],
        axis=1,
    )
    mean = jnp.mean(raw * raw, axis=1, keepdims=True)
    key = (raw * lax.rsqrt(mean + 1e-06)).astype(bf16)
    value = jnp.dot(key, uv_ref[...], preferred_element_type=f32)
    key = key.astype(f32)
    queries = q_ref[...]

    def score(back):
        ropes = sum(pltpu.roll(blocks[g], back, 0) * rope_ref[g] for g in range(groups))
        latent = jnp.sum(pltpu.roll(key, back, 0) * queries, axis=1, keepdims=True)
        return (latent + jnp.sum(ropes, axis=1, keepdims=True)) * scale

    summit = jnp.max(levels, axis=0)
    fresh = []
    for back in range(steps):
        level = jnp.where(row % steps >= back, score(back), MASKED)
        fresh.append((level, pltpu.roll(value, back, 0)))
        summit = jnp.maximum(summit, level)
    factor = jnp.exp(levels - summit[None])
    merged = jnp.sum(pltpu.roll(parts, 4, 1) * factor, axis=0)
    totals = jnp.sum(factor, axis=0)
    for level, values in fresh:
        factor = jnp.exp(level - summit)
        merged += factor * values
        totals += factor
    merged = merged / totals
    for s in range(steps):
        rows = [merged[4 + i * steps + s : 5 + i * steps + s] for i in range(owned)]
        out_ref[s] = jnp.concatenate(rows, axis=0).astype(bf16)


def exchange(array, groups):
    return lax.all_to_all(
        array, "kv", split_axis=0, concat_axis=0, tiled=True, axis_index_groups=groups
    )


def holder(offset, size):
    return offset % RINGS * size + ALONG - 1 + offset // RINGS


def spread_tokens(block, size):
    groups = lax.axis_size("head")
    pairs = [
        (holder(o, size) * groups + (g + o) % groups, holder(o, size) * groups + g)
        for o in range(groups)
        for g in range(groups)
    ]
    return lax.ppermute(block, ("kv", "head"), pairs)


def near(shape, kind):
    return pltpu.VMEM(shape, kind)


def pinned(space, *arrays):
    return [pltpu.with_memory_space_constraint(array, space) for array in arrays]


def limit(mib):
    return pltpu.CompilerParams(vmem_limit_bytes=mib << 20)


def cost(flops, moved):
    return pl.CostEstimate(flops=flops, bytes_accessed=moved, transcendentals=0)


def absorbed(query_nope, uk_weight, copies):
    steps, requests, heads, _ = query_nope.shape
    uk = jnp.swapaxes(uk_weight, 1, 2)
    return pl.pallas_call(
        queries_kernel,
        out_shape=jax.ShapeDtypeStruct((copies, uk.shape[1], steps * requests * heads), bf16),
        in_specs=[HBM, HBM],
        out_specs=VM,
        scratch_shapes=[
            pltpu.VMEM(query_nope.shape, bf16),
            pltpu.VMEM(uk.shape, bf16),
            pltpu.SemaphoreType.DMA((2,)),
        ],
        compiler_params=limit(4),
    )(*pinned(pltpu.HBM, query_nope, uk))


def repeated(columns, shift, copies, *after):
    count, cols, items = columns.shape
    return pl.pallas_call(
        lambda *refs: repeat_kernel(shift, *refs),
        out_shape=jax.ShapeDtypeStruct((copies, count * cols, items), bf16),
        in_specs=[VM] + [pl.BlockSpec(memory_space=pl.ANY)] * len(after),
        out_specs=VM,
        compiler_params=limit(4),
    )(columns, *after)


def prepare(scale, place, lengths, query_rope, cache_rope, cache_latent, uv_weight, lat_new, rope_new, after, groups):
    steps, requests, heads, _ = query_rope.shape
    positions = cache_rope.shape[2]
    return pl.pallas_call(
        lambda *refs: prepare_kernel(scale, *refs),
        out_shape=(
            near((steps * requests * heads, positions), f32),
            near((groups, 8, 128), f32),
            near(cache_latent.shape, bf16),
            near(uv_weight.shape[1:], bf16),
            jax.ShapeDtypeStruct((steps * requests, 128), bf16),
        ),
        in_specs=[SM] + [HBM] * 7 + [pl.BlockSpec(memory_space=pl.ANY)],
        out_specs=(VM,) * 5,
        scratch_shapes=[
            pltpu.SMEM(lengths.shape, jnp.int32),
            pltpu.VMEM(query_rope.shape, bf16),
            pltpu.VMEM(cache_rope.shape, bf16),
            pltpu.VMEM(lat_new.shape, bf16),
            pltpu.VMEM(rope_new.shape, bf16),
            pltpu.SemaphoreType.DMA((7,)),
        ],
        compiler_params=limit(16),
        cost_estimate=cost(1 << 28, 1 << 22),
    )(
        place,
        *pinned(
            pltpu.HBM, lengths, query_rope, cache_rope, cache_latent, uv_weight, lat_new, rope_new
        ),
        after,
    )


def attend(scale, turn, shift, place, queries, keys, bias, uv_weight, token, shards):
    items = bias.shape[0]
    heads, lat, vd = uv_weight.shape
    return pl.pallas_call(
        lambda *refs: attend_kernel(scale, turn, shift, *refs),
        out_shape=(
            jax.ShapeDtypeStruct((shards, 8, vd), bf16),
            jax.ShapeDtypeStruct((8, lat), f32),
        ),
        in_specs=[SM, VM, VM, VM, HBM, VM],
        out_specs=(VM, VM),
        scratch_shapes=[
            pltpu.VMEM((lat // 128, items, 128), f32),
            pltpu.VMEM((items, 128), f32),
            pltpu.VMEM(uv_weight.shape, bf16),
            pltpu.SemaphoreType.DMA,
        ],
        compiler_params=limit(16),
    )(place, queries, *pinned(pltpu.VMEM, keys, bias), *pinned(pltpu.HBM, uv_weight), token)


def merge(scale, shift, place, parts, queries, ropes, uv_own, steps, owned):
    return pl.pallas_call(
        lambda *refs: merge_kernel(scale, shift, *refs),
        out_shape=jax.ShapeDtypeStruct((steps, owned, parts.shape[2]), bf16),
        in_specs=[SM] + [VM] * 4,
        out_specs=VM,
        compiler_params=limit(8),
    )(place, parts, queries, ropes, uv_own)


def on_device(
    query_nope,
    query_rope,
    new_latent,
    new_rope,
    cache_latent,
    cache_rope,
    lengths,
    uk_weight,
    uv_weight,
):
    shards, groups = lax.axis_size("kv"), lax.axis_size("head")
    steps, requests, heads, nope = query_nope.shape
    owned = heads * requests // shards
    scale = mscale / math.sqrt(nope + query_rope.shape[3])
    place = jnp.stack([lax.axis_index("kv"), lax.axis_index("head")]).astype(jnp.int32)
    rings = RINGS
    size = shards // rings
    along = [[r * size + (i + ALONG) % size for i in range(size)] for r in range(rings)]
    across = [[(i + ACROSS) % rings * size + p for i in range(rings)] for p in range(size)]
    everyone = [[(i + ALL) % shards for i in range(shards)]]
    block = absorbed(query_nope, uk_weight, size)
    ring = exchange(block, along)
    bias, ropes, keys, uv_own, mine = prepare(
        scale, place, lengths, query_rope, cache_rope, cache_latent, uv_weight,
        new_latent, new_rope, block, groups,
    )
    token = spread_tokens(mine, size)
    queries = exchange(repeated(ring, ALONG, rings, ropes, token), across)
    parts, own = attend(scale, ACROSS, ALL, place, queries, keys, bias, uv_weight, token, shards)
    parts = exchange(parts, everyone)
    return merge(scale, ALL, place, parts, own, ropes, uv_own, steps, owned)


def solution(mesh):
    return jax.shard_map(
        on_device,
        mesh=mesh,
        in_specs=(
            P(None, None, "head", None),
            P(None, None, "head", None),
            P(None, None, "head"),
            P(None, None, "head"),
            P(None, "kv", None),
            P(None, None, "kv"),
            P(),
            P("head", None, "kv"),
            P("head", None, None),
        ),
        out_specs=P(None, ("head", "kv"), None),
        check_vma=False,
    )
```

```python
import math

import jax
import jax.numpy as jnp
from jax import lax
from jax.experimental import pallas as pl
from jax.experimental.pallas import tpu as pltpu
from jax.sharding import PartitionSpec as P

mscale = (0.1 * math.log(40.0) + 1.0) ** 2
f32 = jnp.float32
bf16 = jnp.bfloat16
MASKED = -1e30
LOWEST = -1e29
VM = pl.BlockSpec(memory_space=pltpu.VMEM)
SM = pl.BlockSpec(memory_space=pltpu.SMEM)
HBM = pl.BlockSpec(memory_space=pltpu.HBM)
RINGS = 4
ALONG, ACROSS, ALL = 10, 2, 40


def fetch(*copies):
    copies = [pltpu.make_async_copy(*copy) for copy in copies]
    for copy in copies:
        copy.start()
    for copy in copies:
        copy.wait()


def queries_kernel(q_hbm, uk_hbm, out_ref, q_ref, uk_ref, sems):
    fetch((uk_hbm, uk_ref, sems.at[0]), (q_hbm, q_ref, sems.at[1]))
    steps, requests, heads, _ = q_ref.shape
    cols = uk_ref.shape[1]
    rows = jnp.concatenate([q_ref[s, b] for b in range(requests) for s in range(steps)], axis=0)
    weights = uk_ref[...].reshape(heads * cols, uk_ref.shape[2])
    every = lax.dot_general(
        weights, rows, (((1,), (1,)), ((), ())), preferred_element_type=f32
    ).reshape(heads, cols, rows.shape[0])
    head_of = lax.broadcasted_iota(jnp.int32, every.shape[1:], 1) % heads
    own = every[0]
    for h in range(1, heads):
        own = jnp.where(head_of == h, every[h], own)
    out_ref[...] = jnp.broadcast_to(own.astype(bf16)[None], out_ref.shape)


def repeat_kernel(shift, in_ref, *refs):
    out_ref = refs[-1]
    count, cols, items = in_ref.shape
    rows = in_ref[...].reshape(count * cols, items)
    first = (count - shift) * cols
    ordered = jnp.concatenate([rows[first:], rows[:first]], axis=0)
    out_ref[...] = jnp.broadcast_to(ordered[None], out_ref.shape)


def put_tokens(lat_ref, rope_ref, out_ref):
    steps, requests, lat = lat_ref.shape
    rope = rope_ref.shape[2]
    rows = steps * requests

    def one_hot(shape, shift):
        return (
            lax.broadcasted_iota(jnp.int32, shape, 1) == lax.broadcasted_iota(jnp.int32, shape, 0) + shift
        ).astype(bf16)

    def joined(ref):
        return jnp.concatenate([ref[t] for t in range(steps)], axis=0)

    placed = jnp.dot(joined(lat_ref), one_hot((lat, 128), 64), preferred_element_type=f32)
    placed += jnp.dot(joined(rope_ref), one_hot((rope, 128), 8), preferred_element_type=f32)
    to = lax.broadcasted_iota(jnp.int32, (rows, rows), 0)
    source = lax.broadcasted_iota(jnp.int32, (rows, rows), 1)
    order = ((to % steps) * requests + to // steps == source).astype(bf16)
    out_ref[...] = jnp.dot(order, placed.astype(bf16), preferred_element_type=f32).astype(bf16)


def own_rows(shard, items, requests, heads, steps):
    row = lax.broadcasted_iota(jnp.int32, (8, items), 0) - 4
    item = lax.broadcasted_iota(jnp.int32, (8, items), 1)
    owned = 4 // steps
    groups = requests // owned
    request = owned * (shard % groups) + row // steps
    wanted = request * (steps * heads) + (row % steps) * heads + shard // groups
    return ((row >= 0) & (item == wanted)).astype(bf16)


def prepare_kernel(
    scale, place_ref, length_hbm, qr_hbm, rope_hbm, keys_hbm, uv_hbm, lat_new_hbm, rope_new_hbm, _,
    bias_ref, own_ref, keys_ref, uv_own_ref, token_ref,
    length_ref, qr_ref, rope_ref, lat_new_ref, rope_new_ref, sems,
):
    steps, requests, heads, ropes = qr_ref.shape
    shard = place_ref[0]
    owner = shard // (requests // (4 // steps))
    pairs = [
        (lat_new_hbm, lat_new_ref), (rope_new_hbm, rope_new_ref), (length_hbm, length_ref),
        (qr_hbm, qr_ref), (rope_hbm, rope_ref), (keys_hbm, keys_ref), (uv_hbm.at[owner], uv_own_ref),
    ]
    copies = [pltpu.make_async_copy(p, q, sems.at[i]) for i, (p, q) in enumerate(pairs)]
    for copy in copies:
        copy.start()
    for copy in copies[:5]:
        copy.wait()
    put_tokens(lat_new_ref, rope_new_ref, token_ref)
    positions = rope_ref.shape[2]
    width = steps * heads
    lane = lax.broadcasted_iota(jnp.int32, (width, positions), 1) + shard * positions
    rows = [
        jnp.concatenate([qr_ref[s, b] for s in range(steps)], axis=0) for b in range(requests)
    ]
    for b in range(requests):
        score = jnp.dot(rows[b], rope_ref[b], preferred_element_type=f32)
        bias_ref[b * width : (b + 1) * width, :] = jnp.where(
            lane < length_ref[b], score * scale, MASKED
        )
    every = jnp.concatenate(rows, axis=0)
    own = own_rows(shard, width * requests, requests, heads, steps)
    mine = jnp.dot(own, every, preferred_element_type=f32).astype(bf16)
    groups = own_ref.shape[0]
    each = ropes // groups
    at = lax.broadcasted_iota(jnp.int32, (ropes, 128), 0)
    to = lax.broadcasted_iota(jnp.int32, (ropes, 128), 1)
    for g in range(groups):
        spread = (at == to - 8 + each * g) & (to >= 8) & (to < 8 + each)
        own_ref[g] = jnp.dot(mine, spread.astype(bf16), preferred_element_type=f32)
    for copy in copies[5:]:
        copy.wait()


def attend_kernel(
    scale, turn, shift, place_ref, q_ref, keys_ref, bias_ref, uv_hbm, token_ref,
    out_ref, own_ref, mix_ref, stat_ref, uv_ref, sem,
):
    copy = pltpu.make_async_copy(uv_hbm, uv_ref, sem)
    copy.start()
    requests, positions, _ = keys_ref.shape
    heads = uv_ref.shape[0]
    items = bias_ref.shape[0]
    width = items // requests
    tile = 128
    per_tile = tile // width
    mine = lax.broadcasted_iota(jnp.int32, (positions, tile), 1) // width
    rows_of = lax.broadcasted_iota(jnp.int32, (tile, tile), 1)
    rings = q_ref.shape[0]
    queries = jnp.concatenate([q_ref[(i - turn) % rings] for i in range(rings)], axis=0)
    for g in range(items // tile):
        q = queries[:, g * tile : (g + 1) * tile]
        scores = None
        for i in range(per_tile):
            part = jnp.dot(keys_ref[g * per_tile + i], q, preferred_element_type=f32)
            scores = part if scores is None else jnp.where(mine == i, part, scores)
        turned = jnp.transpose(scores) * scale + bias_ref[g * tile : (g + 1) * tile, :]
        highest = jnp.maximum(jnp.max(turned, axis=1, keepdims=True), LOWEST)
        weights = jnp.exp(turned - highest).astype(bf16)
        totals = jnp.maximum(jnp.sum(weights.astype(f32), axis=1, keepdims=True), 1e-30)
        level = highest + jnp.log(totals)
        inverse = 1.0 / totals
        high = level.astype(bf16).astype(f32)
        rest = level - high
        middle = rest.astype(bf16).astype(f32)
        low = rest - middle
        stat_ref[g * tile : (g + 1) * tile, :] = jnp.where(
            rows_of == 0, high, jnp.where(rows_of == 1, middle, jnp.where(rows_of == 2, low, 0.0))
        )
        for i in range(per_tile):
            b = g * per_tile + i
            mix = jnp.dot(
                weights[i * width : (i + 1) * width], keys_ref[b], preferred_element_type=f32
            )
            mix = mix * inverse[i * width : (i + 1) * width]
            for c in range(mix_ref.shape[0]):
                mix_ref[c, b * width : (b + 1) * width, :] = mix[:, c * tile : (c + 1) * tile]
    each = items // heads
    own = own_rows(place_ref[0], items, requests, heads, width // heads)
    own_ref[...] = lax.dot_general(
        own, queries, (((1,), (1,)), ((), ())), preferred_element_type=f32
    )
    token = token_ref[...].astype(f32)
    copy.wait()
    upper = lax.broadcasted_iota(jnp.int32, (8, tile), 0) < 4
    shards = out_ref.shape[0]
    for h in range(0, heads, 2):
        mixed = jnp.concatenate(
            [
                jnp.concatenate(
                    [mix_ref[c, pl.ds(i, each, stride=heads), :] for c in range(mix_ref.shape[0])], axis=1
                )
                for i in (h, h + 1)
            ],
            axis=0,
        ).astype(bf16)
        both = jnp.concatenate([uv_ref[h], uv_ref[h + 1]], axis=1)
        result = jnp.dot(mixed, both, preferred_element_type=f32)
        for i in range(2):
            projected = result[i * each : (i + 1) * each, i * tile : (i + 1) * tile]
            stats = stat_ref[pl.ds(h + i, each, stride=heads), :] + token
            for v in range(each // 8):
                p = projected[v * 8 : (v + 1) * 8]
                st = stats[v * 8 : (v + 1) * 8]
                first = (h + i) * (each // 4) + 2 * v
                out_ref[(first - shift) % shards] = jnp.where(upper, p, pltpu.roll(st, 4, 0)).astype(bf16)
                out_ref[(first + 1 - shift) % shards] = jnp.where(upper, pltpu.roll(p, 4, 0), st).astype(bf16)


def merge_kernel(scale, shift, place_ref, parts_ref, q_ref, rope_ref, uv_ref, out_ref):
    steps, owned, _ = out_ref.shape
    groups = rope_ref.shape[0]
    parts = parts_ref[...].astype(f32)
    shards = parts.shape[0]
    lanes = lax.broadcasted_iota(jnp.int32, parts.shape, 2)
    levels = jnp.sum(jnp.where(lanes < 3, parts, 0.0), axis=2, keepdims=True)
    lane = lanes[0]
    row = lax.broadcasted_iota(jnp.int32, (8, 1), 0)
    blocks = [
        parts_ref[
            (holder((g + groups - place_ref[1]) % groups, shards // RINGS) + shards - shift) % shards
        ].astype(f32)
        for g in range(groups)
    ]
    raw = jnp.concatenate(
        [
            jnp.where(lane < 64, pltpu.roll(blocks[g], 64, 1), blocks[g + 1])
            for g in range(0, groups, 2)
        ],
        axis=1,
    )
    mean = jnp.mean(raw * raw, axis=1, keepdims=True)
    key = (raw * lax.rsqrt(mean + 1e-06)).astype(bf16)
    value = jnp.dot(key, uv_ref[...], preferred_element_type=f32)
    key = key.astype(f32)
    queries = q_ref[...]

    def score(back):
        ropes = sum(pltpu.roll(blocks[g], back, 0) * rope_ref[g] for g in range(groups))
        latent = jnp.sum(pltpu.roll(key, back, 0) * queries, axis=1, keepdims=True)
        return (latent + jnp.sum(ropes, axis=1, keepdims=True)) * scale

    summit = jnp.max(levels, axis=0)
    fresh = []
    for back in range(steps):
        level = jnp.where(row % steps >= back, score(back), MASKED)
        fresh.append((level, pltpu.roll(value, back, 0)))
        summit = jnp.maximum(summit, level)
    factor = jnp.exp(levels - summit[None])
    merged = jnp.sum(pltpu.roll(parts, 4, 1) * factor, axis=0)
    totals = jnp.sum(factor, axis=0)
    for level, values in fresh:
        factor = jnp.exp(level - summit)
        merged += factor * values
        totals += factor
    merged = merged / totals
    for s in range(steps):
        rows = [merged[4 + i * steps + s : 5 + i * steps + s] for i in range(owned)]
        out_ref[s] = jnp.concatenate(rows, axis=0).astype(bf16)


def exchange(array, groups):
    return lax.all_to_all(
        array, "kv", split_axis=0, concat_axis=0, tiled=True, axis_index_groups=groups
    )


def holder(offset, size):
    return offset % RINGS * size + ALONG - 1 + offset // RINGS


def spread_tokens(block, size):
    groups = lax.axis_size("head")
    pairs = [
        (holder(o, size) * groups + (g + o) % groups, holder(o, size) * groups + g)
        for o in range(groups)
        for g in range(groups)
    ]
    return lax.ppermute(block, ("kv", "head"), pairs)


def near(shape, kind):
    return pltpu.VMEM(shape, kind)


def pinned(space, *arrays):
    return [pltpu.with_memory_space_constraint(array, space) for array in arrays]


def limit(mib):
    return pltpu.CompilerParams(vmem_limit_bytes=mib << 20)


def cost(flops, moved):
    return pl.CostEstimate(flops=flops, bytes_accessed=moved, transcendentals=0)


def absorbed(query_nope, uk_weight, copies):
    steps, requests, heads, _ = query_nope.shape
    uk = jnp.swapaxes(uk_weight, 1, 2)
    return pl.pallas_call(
        queries_kernel,
        out_shape=jax.ShapeDtypeStruct((copies, uk.shape[1], steps * requests * heads), bf16),
        in_specs=[HBM, HBM],
        out_specs=VM,
        scratch_shapes=[
            pltpu.VMEM(query_nope.shape, bf16),
            pltpu.VMEM(uk.shape, bf16),
            pltpu.SemaphoreType.DMA((2,)),
        ],
        compiler_params=limit(4),
    )(*pinned(pltpu.HBM, query_nope, uk))


def repeated(columns, shift, copies, *after):
    count, cols, items = columns.shape
    return pl.pallas_call(
        lambda *refs: repeat_kernel(shift, *refs),
        out_shape=jax.ShapeDtypeStruct((copies, count * cols, items), bf16),
        in_specs=[VM] + [pl.BlockSpec(memory_space=pl.ANY)] * len(after),
        out_specs=VM,
        compiler_params=limit(4),
    )(columns, *after)


def prepare(scale, place, lengths, query_rope, cache_rope, cache_latent, uv_weight, lat_new, rope_new, after, groups):
    steps, requests, heads, _ = query_rope.shape
    positions = cache_rope.shape[2]
    return pl.pallas_call(
        lambda *refs: prepare_kernel(scale, *refs),
        out_shape=(
            near((steps * requests * heads, positions), f32),
            near((groups, 8, 128), f32),
            near(cache_latent.shape, bf16),
            near(uv_weight.shape[1:], bf16),
            jax.ShapeDtypeStruct((steps * requests, 128), bf16),
        ),
        in_specs=[SM] + [HBM] * 7 + [pl.BlockSpec(memory_space=pl.ANY)],
        out_specs=(VM,) * 5,
        scratch_shapes=[
            pltpu.SMEM(lengths.shape, jnp.int32),
            pltpu.VMEM(query_rope.shape, bf16),
            pltpu.VMEM(cache_rope.shape, bf16),
            pltpu.VMEM(lat_new.shape, bf16),
            pltpu.VMEM(rope_new.shape, bf16),
            pltpu.SemaphoreType.DMA((7,)),
        ],
        compiler_params=limit(16),
        cost_estimate=cost(1 << 28, 1 << 22),
    )(
        place,
        *pinned(
            pltpu.HBM, lengths, query_rope, cache_rope, cache_latent, uv_weight, lat_new, rope_new
        ),
        after,
    )


def attend(scale, turn, shift, place, queries, keys, bias, uv_weight, token, shards):
    items = bias.shape[0]
    heads, lat, vd = uv_weight.shape
    return pl.pallas_call(
        lambda *refs: attend_kernel(scale, turn, shift, *refs),
        out_shape=(
            jax.ShapeDtypeStruct((shards, 8, vd), bf16),
            jax.ShapeDtypeStruct((8, lat), f32),
        ),
        in_specs=[SM, VM, VM, VM, HBM, VM],
        out_specs=(VM, VM),
        scratch_shapes=[
            pltpu.VMEM((lat // 128, items, 128), f32),
            pltpu.VMEM((items, 128), f32),
            pltpu.VMEM(uv_weight.shape, bf16),
            pltpu.SemaphoreType.DMA,
        ],
        compiler_params=limit(16),
    )(place, queries, *pinned(pltpu.VMEM, keys, bias), *pinned(pltpu.HBM, uv_weight), token)


def merge(scale, shift, place, parts, queries, ropes, uv_own, steps, owned):
    return pl.pallas_call(
        lambda *refs: merge_kernel(scale, shift, *refs),
        out_shape=jax.ShapeDtypeStruct((steps, owned, parts.shape[2]), bf16),
        in_specs=[SM] + [VM] * 4,
        out_specs=VM,
        compiler_params=limit(8),
    )(place, parts, queries, ropes, uv_own)


def on_device(
    query_nope,
    query_rope,
    new_latent,
    new_rope,
    cache_latent,
    cache_rope,
    lengths,
    uk_weight,
    uv_weight,
):
    shards, groups = lax.axis_size("kv"), lax.axis_size("head")
    steps, requests, heads, nope = query_nope.shape
    owned = heads * requests // shards
    scale = mscale / math.sqrt(nope + query_rope.shape[3])
    place = jnp.stack([lax.axis_index("kv"), lax.axis_index("head")]).astype(jnp.int32)
    rings = RINGS
    size = shards // rings
    along = [[r * size + (i + ALONG) % size for i in range(size)] for r in range(rings)]
    across = [[(i + ACROSS) % rings * size + p for i in range(rings)] for p in range(size)]
    everyone = [[(i + ALL) % shards for i in range(shards)]]
    block = absorbed(query_nope, uk_weight, size)
    ring = exchange(block, along)
    bias, ropes, keys, uv_own, mine = prepare(
        scale, place, lengths, query_rope, cache_rope, cache_latent, uv_weight,
        new_latent, new_rope, block, groups,
    )
    token = spread_tokens(mine, size)
    queries = exchange(repeated(ring, ALONG, rings, ropes, token), across)
    parts, own = attend(scale, ACROSS, ALL, place, queries, keys, bias, uv_weight, token, shards)
    parts = exchange(parts, everyone)
    return merge(scale, ALL, place, parts, own, ropes, uv_own, steps, owned)


def solution(mesh):
    return jax.shard_map(
        on_device,
        mesh=mesh,
        in_specs=(
            P(None, None, "head", None),
            P(None, None, "head", None),
            P(None, None, "head"),
            P(None, None, "head"),
            P(None, "kv", None),
            P(None, None, "kv"),
            P(),
            P("head", None, "kv"),
            P("head", None, None),
        ),
        out_specs=P(None, ("head", "kv"), None),
        check_vma=False,
    )
```

```python
import math

import jax
import jax.numpy as jnp
from jax import lax
from jax.experimental import pallas as pl
from jax.experimental.pallas import tpu as pltpu
from jax.sharding import PartitionSpec as P

mscale = (0.1 * math.log(40.0) + 1.0) ** 2
f32 = jnp.float32
bf16 = jnp.bfloat16
MASKED = -1e30
LOWEST = -1e29
VM = pl.BlockSpec(memory_space=pltpu.VMEM)
SM = pl.BlockSpec(memory_space=pltpu.SMEM)
HBM = pl.BlockSpec(memory_space=pltpu.HBM)
RINGS = 4
ALONG, ACROSS, ALL = 10, 2, 41


def fetch(*copies):
    copies = [pltpu.make_async_copy(*copy) for copy in copies]
    for copy in copies:
        copy.start()
    for copy in copies:
        copy.wait()


def queries_kernel(q_hbm, uk_hbm, out_ref, q_ref, uk_ref, sems):
    fetch((uk_hbm, uk_ref, sems.at[0]), (q_hbm, q_ref, sems.at[1]))
    steps, requests, heads, _ = q_ref.shape
    cols = uk_ref.shape[1]
    rows = jnp.concatenate([q_ref[s, b] for b in range(requests) for s in range(steps)], axis=0)
    weights = uk_ref[...].reshape(heads * cols, uk_ref.shape[2])
    every = lax.dot_general(
        weights, rows, (((1,), (1,)), ((), ())), preferred_element_type=f32
    ).reshape(heads, cols, rows.shape[0])
    head_of = lax.broadcasted_iota(jnp.int32, every.shape[1:], 1) % heads
    own = every[0]
    for h in range(1, heads):
        own = jnp.where(head_of == h, every[h], own)
    out_ref[...] = jnp.broadcast_to(own.astype(bf16)[None], out_ref.shape)


def repeat_kernel(shift, in_ref, *refs):
    out_ref = refs[-1]
    count, cols, items = in_ref.shape
    rows = in_ref[...].reshape(count * cols, items)
    first = (count - shift) * cols
    ordered = jnp.concatenate([rows[first:], rows[:first]], axis=0)
    out_ref[...] = jnp.broadcast_to(ordered[None], out_ref.shape)


def put_tokens(lat_ref, rope_ref, out_ref):
    steps, requests, lat = lat_ref.shape
    rope = rope_ref.shape[2]
    rows = steps * requests

    def one_hot(shape, shift):
        return (
            lax.broadcasted_iota(jnp.int32, shape, 1) == lax.broadcasted_iota(jnp.int32, shape, 0) + shift
        ).astype(bf16)

    def joined(ref):
        return jnp.concatenate([ref[t] for t in range(steps)], axis=0)

    placed = jnp.dot(joined(lat_ref), one_hot((lat, 128), 64), preferred_element_type=f32)
    placed += jnp.dot(joined(rope_ref), one_hot((rope, 128), 8), preferred_element_type=f32)
    to = lax.broadcasted_iota(jnp.int32, (rows, rows), 0)
    source = lax.broadcasted_iota(jnp.int32, (rows, rows), 1)
    order = ((to % steps) * requests + to // steps == source).astype(bf16)
    out_ref[...] = jnp.dot(order, placed.astype(bf16), preferred_element_type=f32).astype(bf16)


def own_rows(shard, items, requests, heads, steps):
    row = lax.broadcasted_iota(jnp.int32, (8, items), 0) - 4
    item = lax.broadcasted_iota(jnp.int32, (8, items), 1)
    owned = 4 // steps
    groups = requests // owned
    request = owned * (shard % groups) + row // steps
    wanted = request * (steps * heads) + (row % steps) * heads + shard // groups
    return ((row >= 0) & (item == wanted)).astype(bf16)


def prepare_kernel(
    scale, place_ref, length_hbm, qr_hbm, rope_hbm, keys_hbm, uv_hbm, lat_new_hbm, rope_new_hbm, _,
    bias_ref, own_ref, keys_ref, uv_own_ref, token_ref,
    length_ref, qr_ref, rope_ref, lat_new_ref, rope_new_ref, sems,
):
    steps, requests, heads, ropes = qr_ref.shape
    shard = place_ref[0]
    owner = shard // (requests // (4 // steps))
    pairs = [
        (lat_new_hbm, lat_new_ref), (rope_new_hbm, rope_new_ref), (length_hbm, length_ref),
        (qr_hbm, qr_ref), (rope_hbm, rope_ref), (keys_hbm, keys_ref), (uv_hbm.at[owner], uv_own_ref),
    ]
    copies = [pltpu.make_async_copy(p, q, sems.at[i]) for i, (p, q) in enumerate(pairs)]
    for copy in copies:
        copy.start()
    for copy in copies[:5]:
        copy.wait()
    put_tokens(lat_new_ref, rope_new_ref, token_ref)
    positions = rope_ref.shape[2]
    width = steps * heads
    lane = lax.broadcasted_iota(jnp.int32, (width, positions), 1) + shard * positions
    rows = [
        jnp.concatenate([qr_ref[s, b] for s in range(steps)], axis=0) for b in range(requests)
    ]
    for b in range(requests):
        score = jnp.dot(rows[b], rope_ref[b], preferred_element_type=f32)
        bias_ref[b * width : (b + 1) * width, :] = jnp.where(
            lane < length_ref[b], score * scale, MASKED
        )
    every = jnp.concatenate(rows, axis=0)
    own = own_rows(shard, width * requests, requests, heads, steps)
    mine = jnp.dot(own, every, preferred_element_type=f32).astype(bf16)
    groups = own_ref.shape[0]
    each = ropes // groups
    at = lax.broadcasted_iota(jnp.int32, (ropes, 128), 0)
    to = lax.broadcasted_iota(jnp.int32, (ropes, 128), 1)
    for g in range(groups):
        spread = (at == to - 8 + each * g) & (to >= 8) & (to < 8 + each)
        own_ref[g] = jnp.dot(mine, spread.astype(bf16), preferred_element_type=f32)
    for copy in copies[5:]:
        copy.wait()


def attend_kernel(
    scale, turn, shift, place_ref, q_ref, keys_ref, bias_ref, uv_hbm, token_ref,
    out_ref, own_ref, mix_ref, stat_ref, uv_ref, sem,
):
    copy = pltpu.make_async_copy(uv_hbm, uv_ref, sem)
    copy.start()
    requests, positions, _ = keys_ref.shape
    heads = uv_ref.shape[0]
    items = bias_ref.shape[0]
    width = items // requests
    tile = 128
    per_tile = tile // width
    mine = lax.broadcasted_iota(jnp.int32, (positions, tile), 1) // width
    rows_of = lax.broadcasted_iota(jnp.int32, (tile, tile), 1)
    rings = q_ref.shape[0]
    queries = jnp.concatenate([q_ref[(i - turn) % rings] for i in range(rings)], axis=0)
    for g in range(items // tile):
        q = queries[:, g * tile : (g + 1) * tile]
        scores = None
        for i in range(per_tile):
            part = jnp.dot(keys_ref[g * per_tile + i], q, preferred_element_type=f32)
            scores = part if scores is None else jnp.where(mine == i, part, scores)
        turned = jnp.transpose(scores) * scale + bias_ref[g * tile : (g + 1) * tile, :]
        highest = jnp.maximum(jnp.max(turned, axis=1, keepdims=True), LOWEST)
        weights = jnp.exp(turned - highest).astype(bf16)
        totals = jnp.maximum(jnp.sum(weights.astype(f32), axis=1, keepdims=True), 1e-30)
        level = highest + jnp.log(totals)
        inverse = 1.0 / totals
        high = level.astype(bf16).astype(f32)
        rest = level - high
        middle = rest.astype(bf16).astype(f32)
        low = rest - middle
        stat_ref[g * tile : (g + 1) * tile, :] = jnp.where(
            rows_of == 0, high, jnp.where(rows_of == 1, middle, jnp.where(rows_of == 2, low, 0.0))
        )
        for i in range(per_tile):
            b = g * per_tile + i
            mix = jnp.dot(
                weights[i * width : (i + 1) * width], keys_ref[b], preferred_element_type=f32
            )
            mix = mix * inverse[i * width : (i + 1) * width]
            for c in range(mix_ref.shape[0]):
                mix_ref[c, b * width : (b + 1) * width, :] = mix[:, c * tile : (c + 1) * tile]
    each = items // heads
    own = own_rows(place_ref[0], items, requests, heads, width // heads)
    own_ref[...] = lax.dot_general(
        own, queries, (((1,), (1,)), ((), ())), preferred_element_type=f32
    )
    token = token_ref[...].astype(f32)
    copy.wait()
    upper = lax.broadcasted_iota(jnp.int32, (8, tile), 0) < 4
    shards = out_ref.shape[0]
    for h in range(0, heads, 2):
        mixed = jnp.concatenate(
            [
                jnp.concatenate(
                    [mix_ref[c, pl.ds(i, each, stride=heads), :] for c in range(mix_ref.shape[0])], axis=1
                )
                for i in (h, h + 1)
            ],
            axis=0,
        ).astype(bf16)
        both = jnp.concatenate([uv_ref[h], uv_ref[h + 1]], axis=1)
        result = jnp.dot(mixed, both, preferred_element_type=f32)
        for i in range(2):
            projected = result[i * each : (i + 1) * each, i * tile : (i + 1) * tile]
            stats = stat_ref[pl.ds(h + i, each, stride=heads), :] + token
            for v in range(each // 8):
                p = projected[v * 8 : (v + 1) * 8]
                st = stats[v * 8 : (v + 1) * 8]
                first = (h + i) * (each // 4) + 2 * v
                out_ref[(first - shift) % shards] = jnp.where(upper, p, pltpu.roll(st, 4, 0)).astype(bf16)
                out_ref[(first + 1 - shift) % shards] = jnp.where(upper, pltpu.roll(p, 4, 0), st).astype(bf16)


def merge_kernel(scale, shift, place_ref, parts_ref, q_ref, rope_ref, uv_ref, out_ref):
    steps, owned, _ = out_ref.shape
    groups = rope_ref.shape[0]
    parts = parts_ref[...].astype(f32)
    shards = parts.shape[0]
    lanes = lax.broadcasted_iota(jnp.int32, parts.shape, 2)
    levels = jnp.sum(jnp.where(lanes < 3, parts, 0.0), axis=2, keepdims=True)
    lane = lanes[0]
    row = lax.broadcasted_iota(jnp.int32, (8, 1), 0)
    blocks = [
        parts_ref[
            (holder((g + groups - place_ref[1]) % groups, shards // RINGS) + shards - shift) % shards
        ].astype(f32)
        for g in range(groups)
    ]
    raw = jnp.concatenate(
        [
            jnp.where(lane < 64, pltpu.roll(blocks[g], 64, 1), blocks[g + 1])
            for g in range(0, groups, 2)
        ],
        axis=1,
    )
    mean = jnp.mean(raw * raw, axis=1, keepdims=True)
    key = (raw * lax.rsqrt(mean + 1e-06)).astype(bf16)
    value = jnp.dot(key, uv_ref[...], preferred_element_type=f32)
    key = key.astype(f32)
    queries = q_ref[...]

    def score(back):
        ropes = sum(pltpu.roll(blocks[g], back, 0) * rope_ref[g] for g in range(groups))
        latent = jnp.sum(pltpu.roll(key, back, 0) * queries, axis=1, keepdims=True)
        return (latent + jnp.sum(ropes, axis=1, keepdims=True)) * scale

    summit = jnp.max(levels, axis=0)
    fresh = []
    for back in range(steps):
        level = jnp.where(row % steps >= back, score(back), MASKED)
        fresh.append((level, pltpu.roll(value, back, 0)))
        summit = jnp.maximum(summit, level)
    factor = jnp.exp(levels - summit[None])
    merged = jnp.sum(pltpu.roll(parts, 4, 1) * factor, axis=0)
    totals = jnp.sum(factor, axis=0)
    for level, values in fresh:
        factor = jnp.exp(level - summit)
        merged += factor * values
        totals += factor
    merged = merged / totals
    for s in range(steps):
        rows = [merged[4 + i * steps + s : 5 + i * steps + s] for i in range(owned)]
        out_ref[s] = jnp.concatenate(rows, axis=0).astype(bf16)


def exchange(array, groups):
    return lax.all_to_all(
        array, "kv", split_axis=0, concat_axis=0, tiled=True, axis_index_groups=groups
    )


def holder(offset, size):
    return offset % RINGS * size + ALONG - 1 + offset // RINGS


def spread_tokens(block, size):
    groups = lax.axis_size("head")
    pairs = [
        (holder(o, size) * groups + (g + o) % groups, holder(o, size) * groups + g)
        for o in range(groups)
        for g in range(groups)
    ]
    return lax.ppermute(block, ("kv", "head"), pairs)


def near(shape, kind):
    return pltpu.VMEM(shape, kind)


def pinned(space, *arrays):
    return [pltpu.with_memory_space_constraint(array, space) for array in arrays]


def limit(mib):
    return pltpu.CompilerParams(vmem_limit_bytes=mib << 20)


def cost(flops, moved):
    return pl.CostEstimate(flops=flops, bytes_accessed=moved, transcendentals=0)


def absorbed(query_nope, uk_weight, copies):
    steps, requests, heads, _ = query_nope.shape
    uk = jnp.swapaxes(uk_weight, 1, 2)
    return pl.pallas_call(
        queries_kernel,
        out_shape=jax.ShapeDtypeStruct((copies, uk.shape[1], steps * requests * heads), bf16),
        in_specs=[HBM, HBM],
        out_specs=VM,
        scratch_shapes=[
            pltpu.VMEM(query_nope.shape, bf16),
            pltpu.VMEM(uk.shape, bf16),
            pltpu.SemaphoreType.DMA((2,)),
        ],
        compiler_params=limit(4),
    )(*pinned(pltpu.HBM, query_nope, uk))


def repeated(columns, shift, copies, *after):
    count, cols, items = columns.shape
    return pl.pallas_call(
        lambda *refs: repeat_kernel(shift, *refs),
        out_shape=jax.ShapeDtypeStruct((copies, count * cols, items), bf16),
        in_specs=[VM] + [pl.BlockSpec(memory_space=pl.ANY)] * len(after),
        out_specs=VM,
        compiler_params=limit(4),
    )(columns, *after)


def prepare(scale, place, lengths, query_rope, cache_rope, cache_latent, uv_weight, lat_new, rope_new, after, groups):
    steps, requests, heads, _ = query_rope.shape
    positions = cache_rope.shape[2]
    return pl.pallas_call(
        lambda *refs: prepare_kernel(scale, *refs),
        out_shape=(
            near((steps * requests * heads, positions), f32),
            near((groups, 8, 128), f32),
            near(cache_latent.shape, bf16),
            near(uv_weight.shape[1:], bf16),
            jax.ShapeDtypeStruct((steps * requests, 128), bf16),
        ),
        in_specs=[SM] + [HBM] * 7 + [pl.BlockSpec(memory_space=pl.ANY)],
        out_specs=(VM,) * 5,
        scratch_shapes=[
            pltpu.SMEM(lengths.shape, jnp.int32),
            pltpu.VMEM(query_rope.shape, bf16),
            pltpu.VMEM(cache_rope.shape, bf16),
            pltpu.VMEM(lat_new.shape, bf16),
            pltpu.VMEM(rope_new.shape, bf16),
            pltpu.SemaphoreType.DMA((7,)),
        ],
        compiler_params=limit(16),
        cost_estimate=cost(1 << 28, 1 << 22),
    )(
        place,
        *pinned(
            pltpu.HBM, lengths, query_rope, cache_rope, cache_latent, uv_weight, lat_new, rope_new
        ),
        after,
    )


def attend(scale, turn, shift, place, queries, keys, bias, uv_weight, token, shards):
    items = bias.shape[0]
    heads, lat, vd = uv_weight.shape
    return pl.pallas_call(
        lambda *refs: attend_kernel(scale, turn, shift, *refs),
        out_shape=(
            jax.ShapeDtypeStruct((shards, 8, vd), bf16),
            jax.ShapeDtypeStruct((8, lat), f32),
        ),
        in_specs=[SM, VM, VM, VM, HBM, VM],
        out_specs=(VM, VM),
        scratch_shapes=[
            pltpu.VMEM((lat // 128, items, 128), f32),
            pltpu.VMEM((items, 128), f32),
            pltpu.VMEM(uv_weight.shape, bf16),
            pltpu.SemaphoreType.DMA,
        ],
        compiler_params=limit(16),
    )(place, queries, *pinned(pltpu.VMEM, keys, bias), *pinned(pltpu.HBM, uv_weight), token)


def merge(scale, shift, place, parts, queries, ropes, uv_own, steps, owned):
    return pl.pallas_call(
        lambda *refs: merge_kernel(scale, shift, *refs),
        out_shape=jax.ShapeDtypeStruct((steps, owned, parts.shape[2]), bf16),
        in_specs=[SM] + [VM] * 4,
        out_specs=VM,
        compiler_params=limit(8),
    )(place, parts, queries, ropes, uv_own)


def on_device(
    query_nope,
    query_rope,
    new_latent,
    new_rope,
    cache_latent,
    cache_rope,
    lengths,
    uk_weight,
    uv_weight,
):
    shards, groups = lax.axis_size("kv"), lax.axis_size("head")
    steps, requests, heads, nope = query_nope.shape
    owned = heads * requests // shards
    scale = mscale / math.sqrt(nope + query_rope.shape[3])
    place = jnp.stack([lax.axis_index("kv"), lax.axis_index("head")]).astype(jnp.int32)
    rings = RINGS
    size = shards // rings
    along = [[r * size + (i + ALONG) % size for i in range(size)] for r in range(rings)]
    across = [[(i + ACROSS) % rings * size + p for i in range(rings)] for p in range(size)]
    everyone = [[(i + ALL) % shards for i in range(shards)]]
    block = absorbed(query_nope, uk_weight, size)
    ring = exchange(block, along)
    bias, ropes, keys, uv_own, mine = prepare(
        scale, place, lengths, query_rope, cache_rope, cache_latent, uv_weight,
        new_latent, new_rope, block, groups,
    )
    token = spread_tokens(mine, size)
    queries = exchange(repeated(ring, ALONG, rings, ropes, token), across)
    parts, own = attend(scale, ACROSS, ALL, place, queries, keys, bias, uv_weight, token, shards)
    parts = exchange(parts, everyone)
    return merge(scale, ALL, place, parts, own, ropes, uv_own, steps, owned)


def solution(mesh):
    return jax.shard_map(
        on_device,
        mesh=mesh,
        in_specs=(
            P(None, None, "head", None),
            P(None, None, "head", None),
            P(None, None, "head"),
            P(None, None, "head"),
            P(None, "kv", None),
            P(None, None, "kv"),
            P(),
            P("head", None, "kv"),
            P("head", None, None),
        ),
        out_specs=P(None, ("head", "kv"), None),
        check_vma=False,
    )
```
